256 devices in a mesh: ctx: 64 (over z, x, core), head: 4 (over y).
Axes of the slice: x: 4, y: 4, z: 8, core: 2. Of those that a mesh axis runs over, the one named last changes fastest.
Arguments:
- queries: bfloat16 [12288, 16384], P('ctx', 'head'), may hold values from -16 to 16
- keys: bfloat16 [12288, 1024], P('ctx', 'head'), may hold values from -16 to 16
- values: bfloat16 [12288, 1024], P('ctx', 'head'), may hold values from -6 to 6
- doc_lengths: int32 [128], replicated, may hold values from 1 to 2880, 12288 in all
Outputs:
- attended: bfloat16 [12288, 16384], P(('ctx', 'head'))
The draws below stay inside these ranges and needn't reach their ends.
Inputs may be any that keep to these rules, and one draw needn't show every extreme that they name: `doc_lengths`: the longest document has exactly 2880 tokens.
All inputs are finite; a program needn't handle non-finite values.
Results may differ from the reference program's by a relative error of at most 0.0029.
Values may be sent and summed in bfloat16 or wider, within the bound.
A program may use at most 64 MiB of HBM per device.

```python
import math
import jax
import jax.numpy as jnp
import numpy as np
from jax import lax

QUERY_HEADS = 128
KEY_VALUE_HEADS = 8
HEAD_SIZE = 128
TOK_DEV = 192
WINDOW_TOKENS = 12288
HOPS = 16
MOSTDOC = 2880
NDOCS = 128


def draw_keys(key, part):
    key = jax.random.fold_in(key, 11)
    final_output = jax.random.truncated_normal(key, -6.0, 6.0, (WINDOW_TOKENS, KEY_VALUE_HEADS, HEAD_SIZE), jnp.float32)
    return final_output.reshape(WINDOW_TOKENS, KEY_VALUE_HEADS * HEAD_SIZE).astype(jnp.bfloat16)


def draw_queries(key, part):
    key = jax.random.fold_in(key, 12)
    final_output = jax.random.truncated_normal(key, -6.0, 6.0, (WINDOW_TOKENS, KEY_VALUE_HEADS, QUERY_HEADS // KEY_VALUE_HEADS, HEAD_SIZE), jnp.float32)
    return final_output.reshape(WINDOW_TOKENS, QUERY_HEADS * HEAD_SIZE).astype(jnp.bfloat16)


def level_of(stream_key, extent, cuts, smallest, high):
    gain = 1.0
    for axis_at, shards_of in cuts:
        draws = jax.random.uniform(jax.random.fold_in(jax.random.fold_in(stream_key, 6), axis_at), (shards_of,), jnp.float32, smallest / len(cuts), high / len(cuts))
        gain = gain * jnp.repeat(jnp.exp(draws), extent[axis_at] // shards_of).reshape((-1,) + (1,) * (len(extent) - 1 - axis_at))
    return gain


def profile(count, total, bound, slope):
    weights = [(1 << 20) // math.isqrt(grade ** slope) + 1 for grade in range(2, count + 1)]
    rest, given = total - bound - (count - 1), [1] * (count - 1)
    while rest > 0:
        candidates = [i for i in range(count - 1) if given[i] < bound]
        whole, remaining = sum([weights[i] for i in candidates]), rest
        for i in candidates:
            more = min(bound - given[i], max(1, remaining * weights[i] // whole), rest)
            given[i] = given[i] + more
            rest = rest - more
    return np.array([bound] + given)


def uneven(own_key, number_of, total, bound, slope):
    if number_of == 2:
        one = jax.random.randint(own_key, (), max(1, total - bound), min(bound, total - 1) + 1)
        return jnp.stack([one, total - one])
    tallies = jnp.asarray(profile(number_of, total, bound, slope), jnp.int32)
    couples = (number_of - 1) // 2
    giver, taker = tallies[1:1 + 2 * couples:2], tallies[2:2 + 2 * couples:2]
    room = jnp.minimum(giver - 1, bound - taker)
    shifted = jax.random.randint(jax.random.fold_in(own_key, 1), (couples,), 0, 1 << 20) % (room + 1)
    tallies = tallies.at[1:1 + 2 * couples:2].set(giver - shifted).at[2:2 + 2 * couples:2].set(taker + shifted)
    return tallies[jax.random.permutation(jax.random.fold_in(own_key, 2), number_of)]


def scatter_about(rng, dims, deviation, most, cuts=(), kind=jnp.bfloat16):
    factor_of = level_of(rng, dims, cuts, -0.22, 0.18) if cuts else 1.0
    values = jax.random.normal(rng, dims, jnp.float32) * deviation * factor_of
    return jnp.minimum(jnp.maximum(values, -most), most).astype(kind)


def setup_inputs(seed: int = 0) -> dict:
    splits = jax.random.split(jax.random.key(seed), 5)
    queries = draw_queries(jax.random.fold_in(splits[4], 71), 0)
    keys = draw_keys(jax.random.fold_in(splits[4], 71), 0)
    values = scatter_about(splits[2], (WINDOW_TOKENS, KEY_VALUE_HEADS * HEAD_SIZE), 1.0, 6.0, ((0, 64), (1, 4)))
    doc_lengths = uneven(splits[3], NDOCS, WINDOW_TOKENS, MOSTDOC, 2).astype(jnp.int32)
    return dict(queries=queries, keys=keys, values=values, doc_lengths=doc_lengths)


def document_ids(doc_lengths, positions):
    doc_ends = jnp.cumsum(doc_lengths).astype(jnp.int32)
    return jnp.sum((doc_ends[None, :] <= positions[:, None]).astype(jnp.int32), axis=1)


def attend_group(query_part, key_part, value_part, allowed):
    scores = jnp.einsum("qhd,kd->hqk", query_part.astype(jnp.float32), key_part.astype(jnp.float32)) * (HEAD_SIZE ** -0.5)
    scores = jnp.where(allowed[None], scores, -1e30)
    highest = jnp.max(scores, axis=-1, keepdims=True)
    probs = jnp.where(allowed[None], jnp.exp(scores - highest), 0.0)
    totals = jnp.sum(probs, axis=-1)
    rounded = lax.optimization_barrier(probs.astype(jnp.bfloat16))
    mixed = jnp.einsum("hqk,kd->qhd", rounded.astype(jnp.float32), value_part.astype(jnp.float32))
    return (mixed / jnp.transpose(totals)[:, :, None]).astype(jnp.bfloat16)


def reference(queries, keys, values, doc_lengths):
    rows_per_block = math.gcd(512, WINDOW_TOKENS)
    reachable_rows = HOPS * TOK_DEV
    width_of_keys = KEY_VALUE_HEADS * HEAD_SIZE
    positions = jnp.arange(WINDOW_TOKENS, dtype=jnp.int32)
    token_docs = document_ids(doc_lengths, positions)
    padded_key_rows = jnp.concatenate([jnp.zeros((reachable_rows, width_of_keys), keys.dtype), keys])
    padded_value_rows = jnp.concatenate([jnp.zeros((reachable_rows, width_of_keys), values.dtype), values])
    docs_padded = jnp.concatenate([-jnp.ones((reachable_rows,), jnp.int32), token_docs])
    grouped_query_heads = queries.reshape(WINDOW_TOKENS, KEY_VALUE_HEADS, QUERY_HEADS // KEY_VALUE_HEADS, HEAD_SIZE)

    def one_block(block_index):
        leading_entry = (block_index * rows_per_block).astype(jnp.int32)
        query_block = lax.dynamic_slice_in_dim(grouped_query_heads, leading_entry, rows_per_block, 0)
        current_key_block = lax.dynamic_slice_in_dim(padded_key_rows, leading_entry, rows_per_block + reachable_rows, 0).reshape(rows_per_block + reachable_rows, KEY_VALUE_HEADS, HEAD_SIZE)
        current_value_block = lax.dynamic_slice_in_dim(padded_value_rows, leading_entry, rows_per_block + reachable_rows, 0).reshape(rows_per_block + reachable_rows, KEY_VALUE_HEADS, HEAD_SIZE)
        key_docs = lax.dynamic_slice_in_dim(docs_padded, leading_entry, rows_per_block + reachable_rows, 0)
        query_docs = lax.dynamic_slice_in_dim(token_docs, leading_entry, rows_per_block, 0)
        query_pos = leading_entry + jnp.arange(rows_per_block, dtype=jnp.int32)
        key_pos = leading_entry - reachable_rows + jnp.arange(rows_per_block + reachable_rows, dtype=jnp.int32)
        allowed = (key_docs[None, :] == query_docs[:, None]) & (key_pos[None, :] <= query_pos[:, None])

        def one_group(pieces):
            return attend_group(pieces[0], pieces[1], pieces[2], allowed)

        grouped = lax.map(one_group, (jnp.moveaxis(query_block, 1, 0), jnp.moveaxis(current_key_block, 1, 0), jnp.moveaxis(current_value_block, 1, 0)))
        return jnp.moveaxis(grouped, 0, 1).reshape(rows_per_block, QUERY_HEADS * HEAD_SIZE)

    outputs = lax.map(one_block, jnp.arange(WINDOW_TOKENS // rows_per_block, dtype=jnp.int32))
    return outputs.reshape(WINDOW_TOKENS, QUERY_HEADS * HEAD_SIZE)
```

```python
import math

import jax
import jax.numpy as jnp
from jax import lax
from jax.experimental import pallas as pl
from jax.experimental.pallas import tpu as pltpu
from jax.sharding import PartitionSpec as P

HEAD = 128
TOK = 192
GROUPS = 2
PER_GROUP = 16
SLOTS = 16
KEYS = SLOTS * TOK
PART = 4
BLOCKS = GROUPS * PER_GROUP // PART
ROWS = PART * TOK
CHUNK = 1536
EDGE = 256
OWN_TOK = 48
MINUS = -1e30
SCALE = HEAD**-0.5 * math.log2(math.e)
MESH = pl.DeviceIdType.MESH


def rows_of(slot):
    return pl.ds(pl.multiple_of(slot * TOK, TOK), TOK)


def kernel(
    q_hbm, k_hbm, v_hbm, len_ref, out_ref,
    kv, kc, kt, vx, s_ref, qv, ob, start_ref, first_ref, bias_ref,
    in_sem, send_sem, recv_sem, osend_sem, orecv_sem, olocal_sem,
):
    ctx = lax.axis_index("ctx")
    y = lax.axis_index("head")
    z = ctx // 8
    x = lax.rem(ctx // 2, 4)
    c = lax.rem(ctx, 2)
    left, right, across = lax.rem(x + 3, 4), lax.rem(x + 1, 4), lax.rem(x + 2, 4)

    def place(z_at, x_at, c_at):
        return (lax.rem(z_at + 8, 8) * 8 + x_at * 2 + c_at, y)

    sibling = place(z, x, 1 - c)
    up, down = place(z + 1, x, c), place(z - 1, x, c)
    to_left, to_right = place(z, left, c), place(z, right, c)
    over_y = [(ctx, lax.rem(y + r, 4)) for r in (1, 2, 3)]

    loads = []
    for g in range(GROUPS):
        for half, src in ((0, k_hbm), (1, v_hbm)):
            loads.append(pltpu.make_async_copy(
                src.at[:, pl.ds(g * HEAD, HEAD)],
                kv.at[g, pl.ds(0, TOK), pl.ds(half * HEAD, HEAD)],
                in_sem.at[2 * g + half]))
    q_load = pltpu.make_async_copy(q_hbm, qv, in_sem.at[4])
    for load in loads:
        load.start()
    q_load.start()

    barrier = pltpu.get_barrier_semaphore()
    partners = [sibling, up, down, to_left, to_right] + over_y
    for partner in partners:
        pl.semaphore_signal(barrier, inc=1, device_id=partner, device_id_type=MESH)
    pl.semaphore_wait(barrier, len(partners))
    for load in loads:
        load.wait()

    def near(frm, to):
        return lax.rem(2 * (to - frm) + 16, 16)

    def far(frm, to):
        return 8 + 2 * (to - frm)

    def copy(g, index, src, dst, target):
        return pltpu.make_async_remote_copy(
            src_ref=kv.at[g, rows_of(src), :], dst_ref=kv.at[g, rows_of(dst), :],
            send_sem=send_sem.at[g, index], recv_sem=recv_sem.at[g, dst],
            device_id=target, device_id_type=MESH)

    def arrived(g, slot):
        copy(g, 0, slot, slot, sibling).wait_recv()

    step = 1 - 2 * c
    own_or_old_right = jnp.where(x < 3, 0, 16)
    own_or_old_left = jnp.where(x > 0, 16, 0)
    on_right = (c == 0) & (x < 3) | (c == 1) & (x == 2)
    on_left = (c == 0) & (x == 1) | (c == 1) & (x > 0)

    def z_up(g): return copy(g, 0, 0, 8, up)
    def z_on(g): return copy(g, 1, 8, 16, up)
    def near_right(g): return copy(g, 2, own_or_old_right, near(x, right), to_right)
    def near_left(g): return copy(g, 3, own_or_old_left, near(x, left), to_left)
    def far_right(g): return copy(g, 4, 8, far(x, right), to_right)
    def far_left(g): return copy(g, 5, 8, far(x, left), to_left)
    def near_on_right(g): return copy(g, 6, near(left, x), near(left, right), to_right)
    def near_on_left(g): return copy(g, 7, near(right, x), near(right, left), to_left)
    def far_on(g):
        return copy(g, 8, jnp.where(c == 0, far(left, x), far(right, x)),
                    jnp.where(c == 0, far(left, right), far(right, left)),
                    place(z, jnp.where(c == 0, right, left), c))
    def aside(g, index, slot): return copy(g, 9 + index, slot, slot + step, sibling)
    def aside_own(g): return aside(g, 0, 16 * c)

    asides = [8, near(left, x), far(left, x), near(right, x), far(right, x),
              near(across, x), far(across, x)]

    def stage0(g):
        z_up(g).start()

        @pl.when(x < 3)
        def _():
            near_right(g).start()

        @pl.when(x == 0)
        def _():
            near_left(g).start()

        @pl.when(c == 0)
        def _():
            aside_own(g).start()

    def stage1(g):
        arrived(g, 8)
        z_on(g).start()
        far_right(g).start()
        far_left(g).start()
        aside(g, 1, 8).start()

    def stage2(g):
        arrived(g, 16)

        @pl.when(x == 3)
        def _():
            near_right(g).start()

        @pl.when(x > 0)
        def _():
            near_left(g).start()

        @pl.when(c == 1)
        def _():
            aside_own(g).start()

    def stage3(g):
        arrived(g, asides[1])

        @pl.when(on_right)
        def _():
            near_on_right(g).start()
        aside(g, 2, asides[1]).start()
        arrived(g, asides[3])

        @pl.when(on_left)
        def _():
            near_on_left(g).start()
        aside(g, 4, asides[3]).start()
        arrived(g, asides[2])
        arrived(g, asides[4])
        far_on(g).start()
        aside(g, 3, asides[2]).start()
        aside(g, 5, asides[4]).start()

    def stage4(g):
        arrived(g, asides[5])
        aside(g, 6, asides[5]).start()
        arrived(g, asides[6])
        aside(g, 7, asides[6]).start()

    def stage5(g):
        for slot in range(1, 16, 2):
            arrived(g, slot)

    def sent(g):
        for one in (z_up, z_on, near_right, near_left, far_right, far_left, far_on, aside_own):
            one(g).wait_send()

        @pl.when(on_right)
        def _():
            near_on_right(g).wait_send()

        @pl.when(on_left)
        def _():
            near_on_left(g).wait_send()
        for index, slot in enumerate(asides):
            aside(g, 1 + index, slot).wait_send()

    def documents():
        base = ctx * TOK
        lens = jnp.broadcast_to(len_ref[...].astype(jnp.float32), (128, 128))
        row = lax.broadcasted_iota(jnp.int32, (128, 128), 0)
        col = lax.broadcasted_iota(jnp.int32, (128, 128), 1)
        ends = jnp.sum(jnp.where(row <= col, lens.T, 0.0), axis=0, keepdims=True)
        here = (base + lax.broadcasted_iota(jnp.int32, (TOK, 128), 0)).astype(jnp.float32)
        start = jnp.max(jnp.where(ends <= here, ends, 0.0), axis=1, keepdims=True)
        offset = start - base.astype(jnp.float32)
        start_ref[...] = jnp.broadcast_to(offset[:8], (8, 128))
        first = offset < 0.0
        first_ref[...] = jnp.broadcast_to(jnp.where(first, 1.0, 0.0), (TOK, 128))
        i = lax.broadcasted_iota(jnp.int32, (TOK, EDGE), 0)
        j = lax.broadcasted_iota(jnp.int32, (TOK, EDGE), 1)
        inside = (j <= i) & (j.astype(jnp.float32) >= offset)
        rest = jnp.where(first, 0.0, MINUS)
        bias_ref[0] = jnp.where(j < TOK, jnp.where(inside, 0.0, MINUS), rest)
        bias_ref[1] = jnp.broadcast_to(rest, (TOK, EDGE))

    def prepare(g):
        stand_in = kv[g, 0:16, 0:HEAD].astype(jnp.float32)[0:1]
        begin = start_ref[0:1, :]

        def mask_slot(slot, carry):
            at = lax.broadcasted_iota(jnp.int32, (TOK, HEAD), 0) - slot * TOK
            keep = at.astype(jnp.float32) >= begin
            keep = keep | (slot == 0)
            k = kv[g, rows_of(slot), 0:HEAD].astype(jnp.float32)
            v = kv[g, rows_of(slot), HEAD:].astype(jnp.float32)
            kc[rows_of(slot), :] = jnp.where(keep, k, stand_in).astype(jnp.bfloat16)
            vx[g, rows_of(slot), 0:HEAD] = jnp.where(keep, v, 0.0).astype(jnp.bfloat16)
            vx[g, rows_of(slot), HEAD:] = jnp.where(keep, 1.0, 0.0).astype(jnp.bfloat16)
            return carry

        lax.fori_loop(0, SLOTS, mask_slot, 0)

        def turn(tile, carry):
            at = pl.ds(pl.multiple_of(tile * 128, 128), 128)
            turned = kc[at, :].T
            kt[g, 0:HEAD, at] = turned
            kt[g, HEAD:, at] = turned
            return carry

        lax.fori_loop(0, KEYS // 128, turn, 0)

    def out_copies(b):
        at = pl.ds(pl.multiple_of(y * 4096 + b * (PART * HEAD), PART * HEAD), PART * HEAD)
        remote = []
        for r in range(3):
            to = over_y[r]
            remote.append(pltpu.make_async_remote_copy(
                src_ref=ob.at[b, pl.ds(pl.multiple_of(to[1] * OWN_TOK, 16), OWN_TOK), :],
                dst_ref=out_ref.at[:, at],
                send_sem=osend_sem.at[b, r], recv_sem=orecv_sem.at[b, r],
                device_id=to, device_id_type=MESH))
        local = pltpu.make_async_copy(
            ob.at[b, pl.ds(pl.multiple_of(y * OWN_TOK, 16), OWN_TOK), :], out_ref.at[:, at],
            olocal_sem.at[b])
        return remote, local

    def block(b, carry):
        for when, what in ((1, lambda: (stage2(1), stage3(1))), (2, lambda: stage4(1)),
                           (3, lambda: stage5(1)), (4, lambda: prepare(1))):
            @pl.when(b == when)
            def _():
                what()

        g = b // (PER_GROUP // PART)
        parts = []
        for h in range(PART):
            at = pl.ds(pl.multiple_of((b * PART + h) * HEAD, HEAD), HEAD)
            scaled = qv[:, at].astype(jnp.float32) * SCALE
            high = scaled.astype(jnp.bfloat16)
            low = (scaled - high.astype(jnp.float32)).astype(jnp.bfloat16)
            parts.append(jnp.concatenate([high, low], axis=1))
        q = jnp.concatenate(parts, axis=0)
        least = jnp.full((ROWS, 128), MINUS, jnp.float32)

        def score(t, tops):
            edge_top, top = tops
            at = pl.multiple_of(t * CHUNK, CHUNK)
            s = jnp.dot(q, kt[g, :, pl.ds(at, CHUNK)], preferred_element_type=jnp.float32)
            edge = s[:, :EDGE] + jnp.concatenate([bias_ref[t]] * PART, axis=0)
            s_ref[:, pl.ds(at, EDGE)] = edge
            s_ref[:, pl.ds(at + EDGE, CHUNK - EDGE)] = s[:, EDGE:]
            edge_top = jnp.maximum(edge_top, jnp.maximum(edge[:, :128], edge[:, 128:]))
            for u in range(EDGE, CHUNK, 128):
                top = jnp.maximum(top, s[:, u:u + 128])
            return edge_top, top

        edge_top, top = lax.fori_loop(0, KEYS // CHUNK, score, (least, least))
        first = jnp.concatenate([first_ref[...]] * PART, axis=0)[:, :1] > 0.5
        top = jnp.where(first, jnp.max(top, axis=1, keepdims=True), MINUS)
        m = jnp.maximum(jnp.max(edge_top, axis=1, keepdims=True), top)
        m_rest = jnp.where(first, m, -MINUS)

        def mix(t, total):
            at = pl.multiple_of(t * CHUNK, CHUNK)
            edge = jnp.exp2(s_ref[:, pl.ds(at, EDGE)] - m).astype(jnp.bfloat16)
            rest = jnp.exp2(s_ref[:, pl.ds(at + EDGE, CHUNK - EDGE)] - m_rest).astype(jnp.bfloat16)
            p = jnp.concatenate([edge, rest], axis=1)
            return total + jnp.dot(p, vx[g, pl.ds(at, CHUNK), :], preferred_element_type=jnp.float32)

        total = lax.fori_loop(0, KEYS // CHUNK, mix, jnp.zeros((ROWS, 2 * HEAD), jnp.float32))
        o = (total[:, :HEAD] / total[:, HEAD:]).astype(jnp.bfloat16)
        for h in range(PART):
            ob[b, :, h * HEAD:(h + 1) * HEAD] = o[h * TOK:(h + 1) * TOK]
        remote, local = out_copies(b)
        for one in remote:
            one.start()
        local.start()
        return carry

    stage0(0)
    documents()
    stage1(0)
    stage2(0)
    stage3(0)
    stage0(1)
    stage4(0)
    stage1(1)
    stage5(0)
    prepare(0)
    q_load.wait()
    lax.fori_loop(0, BLOCKS, block, 0)

    def finish(b, carry):
        remote, local = out_copies(b)
        for one in remote:
            one.wait()
        local.wait()
        return carry

    lax.fori_loop(0, BLOCKS, finish, 0)
    for g in range(GROUPS):
        sent(g)


def per_device(queries, keys, values, doc_lengths):
    hbm = pl.BlockSpec(memory_space=pl.ANY)
    bf16, f32 = jnp.bfloat16, jnp.float32
    return pl.pallas_call(
        kernel,
        out_shape=jax.ShapeDtypeStruct((OWN_TOK, 4 * queries.shape[1]), bf16),
        in_specs=[hbm, hbm, hbm, pl.BlockSpec(memory_space=pltpu.VMEM)],
        out_specs=hbm,
        scratch_shapes=[
            pltpu.VMEM((GROUPS, (SLOTS + 1) * TOK, 2 * HEAD), bf16),
            pltpu.VMEM((KEYS, HEAD), bf16),
            pltpu.VMEM((GROUPS, 2 * HEAD, KEYS), bf16),
            pltpu.VMEM((GROUPS, KEYS, 2 * HEAD), bf16),
            pltpu.VMEM((ROWS, KEYS), f32),
            pltpu.VMEM((TOK, 4096), bf16),
            pltpu.VMEM((BLOCKS, TOK, PART * HEAD), bf16),
            pltpu.VMEM((8, 128), f32),
            pltpu.VMEM((TOK, 128), f32),
            pltpu.VMEM((KEYS // CHUNK, TOK, EDGE), f32),
            pltpu.SemaphoreType.DMA((5,)),
            pltpu.SemaphoreType.DMA((GROUPS, 17)),
            pltpu.SemaphoreType.DMA((GROUPS, 17)),
            pltpu.SemaphoreType.DMA((BLOCKS, 3)),
            pltpu.SemaphoreType.DMA((BLOCKS, 3)),
            pltpu.SemaphoreType.DMA((BLOCKS,)),
        ],
        compiler_params=pltpu.CompilerParams(
            collective_id=0, has_side_effects=True, vmem_limit_bytes=60 << 20),
    )(queries, keys, values, doc_lengths.reshape(1, 128))


def solution(mesh):
    placed = (P("ctx", "head"), P("ctx", "head"), P("ctx", "head"), P())
    return jax.shard_map(
        per_device, mesh=mesh, in_specs=placed, out_specs=P(("ctx", "head"), None), check_vma=False
    )
```

```python
import math

import jax
import jax.numpy as jnp
from jax import lax
from jax.experimental import pallas as pl
from jax.experimental.pallas import tpu as pltpu
from jax.sharding import PartitionSpec as P

HEAD = 128
TOK = 192
GROUPS = 2
PER_GROUP = 16
SLOTS = 16
KEYS = SLOTS * TOK
PART = 4
PARTS = PER_GROUP // PART
BLOCKS = GROUPS * PARTS
ROWS = PART * TOK
CHUNK = 1536
EDGE = 256
OWN_TOK = 48
MINUS = -1e30
SCALE = HEAD**-0.5 * math.log2(math.e)
MESH = pl.DeviceIdType.MESH


PLANES = 2 * GROUPS


def rows_of(slot):
    return pl.ds(pl.multiple_of(slot * TOK, TOK), TOK)


def kernel(
    q_hbm, k_hbm, v_hbm, len_ref, out_ref,
    kv, kc, kt, vx, s_ref, edge_ref, top_ref, qv, qs, ob, start_ref, first_ref, bias_ref,
    in_sem, send_sem, recv_sem, osend_sem, orecv_sem, olocal_sem,
):
    ctx = lax.axis_index("ctx")
    y = lax.axis_index("head")
    z = ctx // 8
    x = lax.rem(ctx // 2, 4)
    c = lax.rem(ctx, 2)

    def place(z_at, x_at, c_at):
        return (lax.rem(z_at + 8, 8) * 8 + x_at * 2 + c_at, y)

    sibling = place(z, x, 1 - c)
    others = [lax.rem(x + r, 4) for r in (1, 3, 2)]
    over_x = [place(z, to, c) for to in others]
    over_y = [(ctx, lax.rem(y + r, 4)) for r in (1, 2, 3)]
    aslant = [place(jnp.where(to < x, z + 1, z - 1), to, c) for to in others]

    loads = []
    for p in range(PLANES):
        loads.append(pltpu.make_async_copy(
            (k_hbm, v_hbm)[p % 2].at[:, pl.ds(p // 2 * HEAD, HEAD)],
            kv.at[p, pl.ds(0, TOK), :], in_sem.at[p]))
    q_load = pltpu.make_async_copy(q_hbm, qv, in_sem.at[PLANES])
    for load in loads:
        load.start()
    q_load.start()

    barrier = pltpu.get_barrier_semaphore()
    partners = [sibling] + [place(z + r, x, c) for r in (1, 2, -1, -2)] + over_x + over_y + aslant
    for partner in partners:
        pl.semaphore_signal(barrier, inc=1, device_id=partner, device_id_type=MESH)
    pl.semaphore_wait(barrier, len(partners))
    for load in loads:
        load.wait()

    def copy(p, index, src, dst, target):
        return pltpu.make_async_remote_copy(
            src_ref=kv.at[p, rows_of(src), :], dst_ref=kv.at[p, rows_of(dst), :],
            send_sem=send_sem.at[p, index], recv_sem=recv_sem.at[p, dst],
            device_id=target, device_id_type=MESH)

    def arrived(p, slot):
        copy(p, 0, slot, slot, sibling).wait_recv()

    def z_one(p): return copy(p, 0, 0, 8, place(z + 1, x, c))
    def z_two(p): return copy(p, 1, 0, 16, place(z + 2, x, c))

    def even(p, r):
        to = others[r]
        return copy(p, 2 + r, jnp.where(to > x, 0, 16), lax.rem(2 * (to - x) + 16, 16), over_x[r])

    def back(p, r):
        return copy(p, 5 + r, 8, 8 + 2 * (others[r] - x), over_x[r])

    def slanted(p, r):
        return copy(p, 5 + r, 0, 8 + 2 * (others[r] - x), aslant[r])

    def aside(p, slot): return copy(p, 8 + slot // 2, slot, slot + 1 - 2 * c, sibling)
    def aside_own(p): return copy(p, 8, 16 * c, 1 + 14 * c, sibling)

    def send_up(p):
        z_one(p).start()
        z_two(p).start()

    def send_row(p):
        for r in range(3):
            @pl.when(others[r] > x)
            def _():
                even(p, r).start()

        @pl.when(c == 0)
        def _():
            aside_own(p).start()

    def send_slanted(p):
        for r in range(3):
            @pl.when(others[r] < x)
            def _():
                slanted(p, r).start()

    def send_back(p):
        arrived(p, 8)
        for r in range(3):
            if p == 0:
                @pl.when(others[r] > x)
                def _():
                    back(p, r).start()
            else:
                back(p, r).start()
        aside(p, 8).start()

    def send_old(p):
        arrived(p, 16)
        for r in range(3):
            @pl.when(others[r] < x)
            def _():
                even(p, r).start()

        @pl.when(c == 1)
        def _():
            aside_own(p).start()

    def share(p, slots):
        for slot in slots:
            arrived(p, slot)
            aside(p, slot).start()

    def await_odd(p, slots):
        for slot in slots:
            arrived(p, slot)

    def sent(p):
        z_one(p).wait_send()
        z_two(p).wait_send()
        for r in range(3):
            even(p, r).wait_send()
            back(p, r).wait_send()
        aside_own(p).wait_send()
        for slot in range(2, 16, 2):
            aside(p, slot).wait_send()

    def documents():
        base = ctx * TOK
        lens = jnp.broadcast_to(len_ref[...].astype(jnp.float32), (128, 128))
        row = lax.broadcasted_iota(jnp.int32, (128, 128), 0)
        col = lax.broadcasted_iota(jnp.int32, (128, 128), 1)
        ends = jnp.sum(jnp.where(row <= col, lens.T, 0.0), axis=0, keepdims=True)
        here = (base + lax.broadcasted_iota(jnp.int32, (TOK, 128), 0)).astype(jnp.float32)
        start = jnp.max(jnp.where(ends <= here, ends, 0.0), axis=1, keepdims=True)
        offset = start - base.astype(jnp.float32)
        start_ref[...] = jnp.broadcast_to(offset[:8], (8, 128))
        first = offset < 0.0
        first_ref[...] = jnp.broadcast_to(jnp.where(first, 1.0, 0.0), (TOK, 128))
        i = lax.broadcasted_iota(jnp.int32, (TOK, EDGE), 0)
        j = lax.broadcasted_iota(jnp.int32, (TOK, EDGE), 1)
        inside = (j <= i) & (j.astype(jnp.float32) >= offset)
        rest = jnp.where(first, 0.0, MINUS)
        bias_ref[0] = jnp.where(j < TOK, jnp.where(inside, 0.0, MINUS), rest)
        bias_ref[1] = jnp.broadcast_to(rest, (TOK, EDGE))

    def scale_queries():
        def one(h, carry):
            scaled = qv[:, pl.ds(pl.multiple_of(h * HEAD, HEAD), HEAD)].astype(jnp.float32) * SCALE
            high = scaled.astype(jnp.bfloat16)
            qs[rows_of(h), 0:HEAD] = high
            qs[rows_of(h), HEAD:] = (scaled - high.astype(jnp.float32)).astype(jnp.bfloat16)
            return carry

        lax.fori_loop(0, GROUPS * PER_GROUP, one, 0)

    def kept(slot):
        at = lax.broadcasted_iota(jnp.int32, (TOK, HEAD), 0) - slot * TOK
        return (at.astype(jnp.float32) >= start_ref[0:1, :]) | (slot == 0)

    def prepare_keys(g, half):
        p = 2 * g
        stand_in = kv[p, 0:16, :].astype(jnp.float32)[0:1]

        def mask_slot(slot, carry):
            k = kv[p, rows_of(slot), :].astype(jnp.float32)
            kc[rows_of(slot), :] = jnp.where(kept(slot), k, stand_in).astype(jnp.bfloat16)
            return carry

        lax.fori_loop(half * 8, half * 8 + 8, mask_slot, 0)

        def turn(tile, carry):
            at = pl.ds(pl.multiple_of(tile * 128, 128), 128)
            turned = kc[at, :].T
            kt[g, 0:HEAD, at] = turned
            kt[g, HEAD:, at] = turned
            return carry

        lax.fori_loop(half * 12, half * 12 + 12, turn, 0)

    def prepare_values(g):
        def mask_slot(slot, carry):
            keep = kept(slot)
            v = kv[2 * g + 1, rows_of(slot), :].astype(jnp.float32)
            vx[g, rows_of(slot), 0:HEAD] = jnp.where(keep, v, 0.0).astype(jnp.bfloat16)
            vx[g, rows_of(slot), HEAD:] = jnp.where(keep, 1.0, 0.0).astype(jnp.bfloat16)
            return carry

        lax.fori_loop(0, SLOTS, mask_slot, 0)

    def out_copies(b):
        at = pl.ds(pl.multiple_of(y * 4096 + b * (PART * HEAD), PART * HEAD), PART * HEAD)
        remote = []
        for r in range(3):
            to = over_y[r]
            remote.append(pltpu.make_async_remote_copy(
                src_ref=ob.at[b, pl.ds(pl.multiple_of(to[1] * OWN_TOK, 16), OWN_TOK), :],
                dst_ref=out_ref.at[:, at],
                send_sem=osend_sem.at[b, r], recv_sem=orecv_sem.at[b, r],
                device_id=to, device_id_type=MESH))
        local = pltpu.make_async_copy(
            ob.at[b, pl.ds(pl.multiple_of(y * OWN_TOK, 16), OWN_TOK), :], out_ref.at[:, at],
            olocal_sem.at[b])
        return remote, local

    def score(b, t):
        g = b // PARTS
        kept_at = lax.rem(b, PARTS)
        into = jnp.where(t == 0, kept_at, PARTS)
        at = pl.multiple_of(t * CHUNK, CHUNK)
        q = qs[pl.ds(pl.multiple_of(b * ROWS, ROWS), ROWS), :]
        s = jnp.dot(q, kt[g, :, pl.ds(at, CHUNK)], preferred_element_type=jnp.float32)
        edge = s[:, :EDGE] + jnp.concatenate([bias_ref[t]] * PART, axis=0)
        s_ref[into, :, 0:EDGE] = edge
        s_ref[into, :, EDGE:] = s[:, EDGE:]
        edge_ref[t, kept_at] = jnp.maximum(edge[:, :128], edge[:, 128:])
        top = s[:, EDGE:EDGE + 128]
        for u in range(EDGE + 128, CHUNK, 128):
            top = jnp.maximum(top, s[:, u:u + 128])
        top_ref[t, kept_at] = top

    def near_scores(b, carry):
        for when, what in NEAR_STEPS:
            @pl.when(b == when)
            def _():
                what()
        score(b, 0)
        return carry

    def block(b, carry):
        for when, what in STEPS:
            @pl.when(b == when)
            def _():
                what()
        g = b // PARTS
        kept_at = lax.rem(b, PARTS)

        def score_on(t, carry):
            score(b, t)
            return carry

        lax.fori_loop(jnp.where(b < PARTS, 1, 0), 2, score_on, 0)
        for when, what in VALUE_STEPS:
            @pl.when(b == when)
            def _():
                what()
        first = jnp.concatenate([first_ref[...]] * PART, axis=0)[:, :1] > 0.5
        top = jnp.max(jnp.maximum(top_ref[0, kept_at], top_ref[1, kept_at]), axis=1, keepdims=True)
        edge_top = jnp.max(jnp.maximum(edge_ref[0, kept_at], edge_ref[1, kept_at]), axis=1, keepdims=True)
        m = jnp.maximum(edge_top, jnp.where(first, top, MINUS))
        m_rest = jnp.where(first, m, -MINUS)

        def mix(t, total):
            at = pl.multiple_of(t * CHUNK, CHUNK)
            frm = jnp.where(t == 0, kept_at, PARTS)
            edge = jnp.exp2(s_ref[frm, :, 0:EDGE] - m).astype(jnp.bfloat16)
            rest = jnp.exp2(s_ref[frm, :, EDGE:] - m_rest).astype(jnp.bfloat16)
            p = jnp.concatenate([edge, rest], axis=1)
            return total + jnp.dot(p, vx[g, pl.ds(at, CHUNK), :], preferred_element_type=jnp.float32)

        total = lax.fori_loop(0, 2, mix, jnp.zeros((ROWS, 2 * HEAD), jnp.float32))
        o = (total[:, :HEAD] / total[:, HEAD:]).astype(jnp.bfloat16)
        for h in range(PART):
            ob[b, :, h * HEAD:(h + 1) * HEAD] = o[h * TOK:(h + 1) * TOK]
        remote, local = out_copies(b)
        for one in remote:
            one.start()
        local.start()
        return carry

    near, far = (2, 4, 6), (10, 12, 14)
    odd_near, odd_far = (1, 3, 5, 7), (9, 11, 13, 15)
    NEAR_STEPS = (
        (1, lambda: share(0, far)),
        (2, lambda: send_up(2)),
        (3, lambda: send_row(2)),
    )
    STEPS = (
        (0, lambda: (share(1, near + far), await_odd(0, odd_far), prepare_keys(0, 1))),
        (1, lambda: (send_old(2), send_up(3))),
        (2, lambda: (send_row(3), send_back(3))),
        (3, lambda: await_odd(2, odd_near + odd_far)),
        (4, lambda: (prepare_keys(1, 0), prepare_keys(1, 1), share(3, near + far))),
    )
    VALUE_STEPS = (
        (0, lambda: (send_back(2), await_odd(1, odd_near + odd_far), prepare_values(0))),
        (2, lambda: (share(2, near + far), send_old(3))),
        (4, lambda: (await_odd(3, odd_near + odd_far), prepare_values(1))),
    )

    send_row(0)
    send_slanted(0)
    send_up(0)
    send_up(1)
    documents()
    q_load.wait()
    scale_queries()
    share(0, near)
    send_back(0)
    send_old(0)
    send_row(1)
    send_back(1)
    send_old(1)
    await_odd(0, odd_near)
    prepare_keys(0, 0)
    lax.fori_loop(0, PARTS, near_scores, 0)
    lax.fori_loop(0, BLOCKS, block, 0)

    def finish(b, carry):
        remote, local = out_copies(b)
        for one in remote:
            one.wait()
        local.wait()
        return carry

    lax.fori_loop(0, BLOCKS, finish, 0)
    for p in range(PLANES):
        sent(p)


def per_device(queries, keys, values, doc_lengths):
    hbm = pl.BlockSpec(memory_space=pl.ANY)
    bf16, f32 = jnp.bfloat16, jnp.float32
    return pl.pallas_call(
        kernel,
        out_shape=jax.ShapeDtypeStruct((OWN_TOK, 4 * queries.shape[1]), bf16),
        in_specs=[hbm, hbm, hbm, pl.BlockSpec(memory_space=pltpu.VMEM)],
        out_specs=hbm,
        scratch_shapes=[
            pltpu.VMEM((PLANES, (SLOTS + 1) * TOK, HEAD), bf16),
            pltpu.VMEM((KEYS, HEAD), bf16),
            pltpu.VMEM((GROUPS, 2 * HEAD, KEYS), bf16),
            pltpu.VMEM((GROUPS, KEYS, 2 * HEAD), bf16),
            pltpu.VMEM((PARTS + 1, ROWS, CHUNK), f32),
            pltpu.VMEM((2, PARTS, ROWS, 128), f32),
            pltpu.VMEM((2, PARTS, ROWS, 128), f32),
            pltpu.VMEM((TOK, 4096), bf16),
            pltpu.VMEM((GROUPS * PER_GROUP * TOK, 2 * HEAD), bf16),
            pltpu.VMEM((BLOCKS, TOK, PART * HEAD), bf16),
            pltpu.VMEM((8, 128), f32),
            pltpu.VMEM((TOK, 128), f32),
            pltpu.VMEM((2, TOK, EDGE), f32),
            pltpu.SemaphoreType.DMA((PLANES + 1,)),
            pltpu.SemaphoreType.DMA((PLANES, 16)),
            pltpu.SemaphoreType.DMA((PLANES, SLOTS + 1)),
            pltpu.SemaphoreType.DMA((BLOCKS, 3)),
            pltpu.SemaphoreType.DMA((BLOCKS, 3)),
            pltpu.SemaphoreType.DMA((BLOCKS,)),
        ],
        compiler_params=pltpu.CompilerParams(
            collective_id=0, has_side_effects=True, vmem_limit_bytes=60 << 20),
    )(queries, keys, values, doc_lengths.reshape(1, 128))


def solution(mesh):
    placed = (P("ctx", "head"), P("ctx", "head"), P("ctx", "head"), P())
    return jax.shard_map(
        per_device, mesh=mesh, in_specs=placed, out_specs=P(("ctx", "head"), None), check_vma=False
    )
```

```python
import math

import jax
import jax.numpy as jnp
from jax import lax
from jax.experimental import pallas as pl
from jax.experimental.pallas import tpu as pltpu
from jax.sharding import PartitionSpec as P

HEAD = 128
TOK = 192
GROUPS = 2
PER_GROUP = 16
SLOTS = 16
KEYS = SLOTS * TOK
PART = 4
PARTS = PER_GROUP // PART
BLOCKS = GROUPS * PARTS
ROWS = PART * TOK
CHUNK = 1536
EDGE = 256
OWN_TOK = 48
MINUS = -1e30
SCALE = HEAD**-0.5 * math.log2(math.e)
MESH = pl.DeviceIdType.MESH


PLANES = 2 * GROUPS


def rows_of(slot):
    return pl.ds(pl.multiple_of(slot * TOK, TOK), TOK)


def kernel(
    q_hbm, k_hbm, v_hbm, len_ref, out_ref,
    kv, s_ref, top_ref, m_ref, near_ref, qv, qs, ob, row_bias_ref, key_bias_ref, bias_ref,
    in_sem, above_sem, send_sem, recv_sem, osend_sem, orecv_sem, olocal_sem,
):
    ctx = lax.axis_index("ctx")
    y = lax.axis_index("head")
    z = ctx // 8
    x = lax.rem(ctx // 2, 4)
    c = lax.rem(ctx, 2)

    def place(z_at, x_at, c_at):
        return (lax.rem(z_at + 8, 8) * 8 + x_at * 2 + c_at, y)

    sibling = place(z, x, 1 - c)
    others = [lax.rem(x + r, 4) for r in (1, 3, 2)]
    over_x = [place(z, to, c) for to in others]
    over_y = [(ctx, lax.rem(y + r, 4)) for r in (1, 2, 3)]
    loads = []
    for p in range(PLANES):
        loads.append(pltpu.make_async_copy(
            (k_hbm, v_hbm)[p % 2].at[:, pl.ds(p // 2 * HEAD, HEAD)],
            kv.at[p, pl.ds(0, TOK), :], in_sem.at[p]))
    q_load = pltpu.make_async_copy(q_hbm, qv, in_sem.at[PLANES])
    for load in loads:
        load.start()
    q_load.start()

    barrier = pltpu.get_barrier_semaphore()
    above, below = place(z + 1, x, c), place(z - 1, x, c)
    has_above, has_below = z < 7, z > 0
    partners = [sibling] + over_x + over_y
    for partner in partners:
        pl.semaphore_signal(barrier, inc=1, device_id=partner, device_id_type=MESH)

    @pl.when(has_above)
    def _():
        pl.semaphore_signal(barrier, inc=1, device_id=above, device_id_type=MESH)

    pl.semaphore_wait(barrier, len(partners) + jnp.where(has_below, 1, 0))

    @pl.when(has_below)
    def _():
        pl.semaphore_signal(above_sem, inc=1, device_id=below, device_id_type=MESH)

    for load in loads:
        load.wait()

    def copy(p, index, src, dst, target):
        return pltpu.make_async_remote_copy(
            src_ref=kv.at[p, rows_of(src), :], dst_ref=kv.at[p, rows_of(dst), :],
            send_sem=send_sem.at[p, index], recv_sem=recv_sem.at[p, dst],
            device_id=target, device_id_type=MESH)

    def arrived(p, slot):
        copy(p, 0, slot, slot, sibling).wait_recv()

    def z_one(p): return copy(p, 0, 0, 8, above)
    def z_two(p): return copy(p, 1, 8, 16, above)

    def even(p, r):
        to = others[r]
        return copy(p, 2 + r, jnp.where(to > x, 0, 16), lax.rem(2 * (to - x) + 16, 16), over_x[r])

    def back(p, r):
        return copy(p, 5 + r, 8, 8 + 2 * (others[r] - x), over_x[r])

    def aside(p, slot): return copy(p, 8 + slot // 2, slot, slot + 1 - 2 * c, sibling)
    def aside_own(p): return copy(p, 8, 16 * c, 1 + 14 * c, sibling)

    def send_up(*planes):
        @pl.when(has_above)
        def _():
            for p in planes:
                z_one(p).start()

    def send_row(p):
        for r in range(3):
            @pl.when(others[r] > x)
            def _():
                even(p, r).start()

        @pl.when(c == 0)
        def _():
            aside_own(p).start()

    def pass_up(p):
        @pl.when(has_below)
        def _():
            arrived(p, 8)

            @pl.when(has_above)
            def _():
                z_two(p).start()

    def back_near(p):
        @pl.when(has_below)
        def _():
            for r in range(3):
                @pl.when(others[r] < x)
                def _():
                    back(p, r).start()
            aside(p, 8).start()

    def back_far(p):
        @pl.when(has_below)
        def _():
            for r in range(3):
                @pl.when(others[r] > x)
                def _():
                    back(p, r).start()

    def send_old(p):
        @pl.when(z > 1)
        def _():
            arrived(p, 16)
            for r in range(3):
                @pl.when(others[r] < x)
                def _():
                    even(p, r).start()

            @pl.when(c == 1)
            def _():
                aside_own(p).start()

    def share(p, slots):
        for slot in slots:
            @pl.when(ctx >= slot)
            def _():
                arrived(p, slot)
                aside(p, slot).start()

    def await_odd(p, slots):
        for slot in slots:
            @pl.when(ctx >= slot)
            def _():
                arrived(p, slot)

    def sent(p):
        @pl.when(has_above)
        def _():
            z_one(p).wait_send()

        @pl.when(has_above & has_below)
        def _():
            z_two(p).wait_send()

        @pl.when(has_below)
        def _():
            for r in range(3):
                back(p, r).wait_send()
        for r in range(3):
            @pl.when((others[r] > x) | (z > 1))
            def _():
                even(p, r).wait_send()

        @pl.when((c == 0) | (z > 1))
        def _():
            aside_own(p).wait_send()
        for slot in range(2, 16, 2):
            @pl.when(ctx >= slot)
            def _():
                aside(p, slot).wait_send()

    def documents():
        base = ctx * TOK
        lens = jnp.broadcast_to(len_ref[...].astype(jnp.float32), (128, 128))
        row = lax.broadcasted_iota(jnp.int32, (128, 128), 0)
        col = lax.broadcasted_iota(jnp.int32, (128, 128), 1)
        ends = jnp.sum(jnp.where(row <= col, lens.T, 0.0), axis=0, keepdims=True)
        here = (base + lax.broadcasted_iota(jnp.int32, (TOK, 128), 0)).astype(jnp.float32)
        start = jnp.max(jnp.where(ends <= here, ends, 0.0), axis=1, keepdims=True)
        offset = start - base.astype(jnp.float32)
        rest = jnp.broadcast_to(jnp.where(offset < 0.0, 0.0, MINUS), (TOK, 128))
        row_bias_ref[...] = rest
        col = lax.broadcasted_iota(jnp.int32, (8, KEYS), 1)
        slot = col // TOK
        at = (col - 2 * TOK * slot).astype(jnp.float32)
        key_bias_ref[...] = jnp.where(at >= offset[:8], 0.0, MINUS)[0:1]
        i = lax.broadcasted_iota(jnp.int32, (TOK, EDGE), 0)
        j = lax.broadcasted_iota(jnp.int32, (TOK, EDGE), 1)
        inside = (j <= i) & (j.astype(jnp.float32) >= offset)
        rest = jnp.concatenate([rest, rest], axis=1) + key_bias_ref[:, :EDGE]
        bias_ref[...] = jnp.where(j < TOK, jnp.where(inside, 0.0, MINUS), rest)

    def clear():
        def one(slot, carry):
            @pl.when(ctx < slot)
            def _():
                for p in range(PLANES):
                    kv[p, rows_of(slot), :] = jnp.zeros((TOK, HEAD), jnp.bfloat16)
            return carry

        lax.fori_loop(1, SLOTS, one, 0)

    def scale_queries():
        def one(h, carry):
            scaled = qv[:, pl.ds(pl.multiple_of(h * HEAD, HEAD), HEAD)].astype(jnp.float32) * SCALE
            high = scaled.astype(jnp.bfloat16)
            qs[rows_of(h), 0:HEAD] = high
            qs[rows_of(h), HEAD:] = (scaled - high.astype(jnp.float32)).astype(jnp.bfloat16)
            return carry

        lax.fori_loop(0, GROUPS * PER_GROUP, one, 0)

    def out_copies(b):
        at = pl.ds(pl.multiple_of(y * 4096 + b * (PART * HEAD), PART * HEAD), PART * HEAD)
        remote = []
        for r in range(3):
            to = over_y[r]
            remote.append(pltpu.make_async_remote_copy(
                src_ref=ob.at[b, pl.ds(pl.multiple_of(to[1] * OWN_TOK, 16), OWN_TOK), :],
                dst_ref=out_ref.at[:, at],
                send_sem=osend_sem.at[b, r], recv_sem=orecv_sem.at[b, r],
                device_id=to, device_id_type=MESH))
        local = pltpu.make_async_copy(
            ob.at[b, pl.ds(pl.multiple_of(y * OWN_TOK, 16), OWN_TOK), :], out_ref.at[:, at],
            olocal_sem.at[b])
        return remote, local

    def score(b, t):
        g = b // PARTS
        kept_at = lax.rem(b, PARTS)
        into = kept_at if t == 0 else PARTS
        q = qs[pl.ds(pl.multiple_of(b * ROWS, ROWS), ROWS), :]
        k = kv[2 * g, t * CHUNK:(t + 1) * CHUNK, :]
        k = jnp.concatenate([k, k], axis=1)
        s = lax.dot_general(q, k, (((1,), (1,)), ((), ())), preferred_element_type=jnp.float32)
        row_bias = jnp.concatenate([row_bias_ref[...]] * PART, axis=0)
        if t == 0:
            edge_bias = jnp.concatenate([bias_ref[...]] * PART, axis=0)
            top = jnp.full((ROWS, 128), MINUS, jnp.float32)
        else:
            top = top_ref[kept_at]
        for u in range(0, CHUNK, 128):
            if t == 0 and u < EDGE:
                bias = edge_bias[:, u:u + 128]
            else:
                bias = row_bias + key_bias_ref[:, t * CHUNK + u:t * CHUNK + u + 128]
            masked = s[:, u:u + 128] + bias
            s_ref[into, :, u:u + 128] = masked
            top = jnp.maximum(top, masked)
        top_ref[kept_at] = top

    def mixed(g, t, frm, m):
        p = jnp.exp2(s_ref[frm] - m).astype(jnp.bfloat16)
        v = kv[2 * g + 1, pl.ds(pl.multiple_of(t * CHUNK, CHUNK), CHUNK), :]
        v = jnp.concatenate([v, jnp.ones_like(v)], axis=1)
        return jnp.dot(p, v, preferred_element_type=jnp.float32)

    def steps(b, table):
        for when, what in table:
            @pl.when(b == when)
            def _():
                what()

    def near_scores(b, carry):
        steps(b, SCORE_STEPS)
        score(b, 0)
        return carry

    def near_mix(b, carry):
        steps(b, MIX_STEPS)
        m = jnp.max(top_ref[b], axis=1, keepdims=True)
        m_ref[b] = jnp.broadcast_to(m, (ROWS, 128))
        near_ref[b] = mixed(0, 0, b, m)
        return carry

    def block(b, carry):
        steps(b, STEPS)
        g = b // PARTS
        kept_at = lax.rem(b, PARTS)

        @pl.when(b >= PARTS)
        def _():
            score(b, 0)
        score(b, 1)
        steps(b, VALUE_STEPS)
        m = jnp.max(top_ref[kept_at], axis=1, keepdims=True)
        before = near_ref[kept_at] * jnp.exp2(m_ref[kept_at] - m)[:, :1]

        def mix(t, total):
            return total + mixed(g, t, jnp.where(t == 0, kept_at, PARTS), m)

        total = lax.fori_loop(
            jnp.where(b < PARTS, 1, 0), 2, mix, jnp.where(b < PARTS, before, 0.0))
        o = (total[:, :HEAD] / total[:, HEAD:]).astype(jnp.bfloat16)
        for h in range(PART):
            ob[b, :, h * HEAD:(h + 1) * HEAD] = o[h * TOK:(h + 1) * TOK]
        remote, local = out_copies(b)
        for one in remote:
            one.start()
        local.start()
        return carry

    near, far = (2, 4, 6), (10, 12, 14)
    odd_near, odd_far = (1, 3, 5, 7), (9, 11, 13, 15)
    SCORE_STEPS = (
        (0, lambda: send_up(2, 3)),
        (1, lambda: (pass_up(1), back_near(1), back_far(0))),
        (2, lambda: send_old(0)),
        (3, lambda: (share(1, near), back_far(1))),
    )
    MIX_STEPS = (
        (0, lambda: (pass_up(2), await_odd(1, odd_near))),
        (1, lambda: (pass_up(3), send_old(1), share(0, far))),
        (3, lambda: (share(1, far), send_row(2), back_near(2), back_far(2))),
    )
    STEPS = (
        (0, lambda: (await_odd(0, odd_far), send_old(2))),
        (1, lambda: send_old(3)),
        (2, lambda: share(2, near + far)),
        (3, lambda: share(3, near + far)),
        (4, lambda: await_odd(2, odd_near + odd_far)),
    )
    VALUE_STEPS = (
        (0, lambda: (await_odd(1, odd_far), send_row(3), back_near(3), back_far(3))),
        (4, lambda: await_odd(3, odd_near + odd_far)),
    )

    send_row(0)
    documents()
    clear()

    @pl.when(has_above)
    def _():
        pl.semaphore_wait(above_sem, 1)

    send_up(0, 1)
    q_load.wait()
    scale_queries()
    pass_up(0)
    back_near(0)
    send_row(1)
    share(0, near)
    await_odd(0, odd_near)
    lax.fori_loop(0, PARTS, near_scores, 0)
    lax.fori_loop(0, PARTS, near_mix, 0)
    lax.fori_loop(0, BLOCKS, block, 0)

    def finish(b, carry):
        remote, local = out_copies(b)
        for one in remote:
            one.wait()
        local.wait()
        return carry

    lax.fori_loop(0, BLOCKS, finish, 0)
    for p in range(PLANES):
        sent(p)


def per_device(queries, keys, values, doc_lengths):
    hbm = pl.BlockSpec(memory_space=pl.ANY)
    bf16, f32 = jnp.bfloat16, jnp.float32
    return pl.pallas_call(
        kernel,
        out_shape=pltpu.VMEM((OWN_TOK, 4 * queries.shape[1]), bf16),
        in_specs=[hbm, hbm, hbm, pl.BlockSpec(memory_space=pltpu.VMEM)],
        out_specs=pl.BlockSpec(memory_space=pltpu.VMEM),
        scratch_shapes=[
            pltpu.VMEM((PLANES, (SLOTS + 1) * TOK, HEAD), bf16),
            pltpu.VMEM((PARTS + 1, ROWS, CHUNK), f32),
            pltpu.VMEM((PARTS, ROWS, 128), f32),
            pltpu.VMEM((PARTS, ROWS, 128), f32),
            pltpu.VMEM((PARTS, ROWS, 2 * HEAD), f32),
            pltpu.VMEM((TOK, 4096), bf16),
            pltpu.VMEM((GROUPS * PER_GROUP * TOK, 2 * HEAD), bf16),
            pltpu.VMEM((BLOCKS, TOK, PART * HEAD), bf16),
            pltpu.VMEM((TOK, 128), f32),
            pltpu.VMEM((1, KEYS), f32),
            pltpu.VMEM((TOK, EDGE), f32),
            pltpu.SemaphoreType.DMA((PLANES + 1,)),
            pltpu.SemaphoreType.REGULAR,
            pltpu.SemaphoreType.DMA((PLANES, 16)),
            pltpu.SemaphoreType.DMA((PLANES, SLOTS + 1)),
            pltpu.SemaphoreType.DMA((BLOCKS, 3)),
            pltpu.SemaphoreType.DMA((BLOCKS, 3)),
            pltpu.SemaphoreType.DMA((BLOCKS,)),
        ],
        compiler_params=pltpu.CompilerParams(
            collective_id=0, has_side_effects=True, vmem_limit_bytes=56 << 20),
    )(queries, keys, values, doc_lengths.reshape(1, 128))


def solution(mesh):
    placed = (P("ctx", "head"), P("ctx", "head"), P("ctx", "head"), P())
    return jax.shard_map(
        per_device, mesh=mesh, in_specs=placed, out_specs=P(("ctx", "head"), None), check_vma=False
    )
```

```python
import math

import jax
import jax.numpy as jnp
from jax import lax
from jax.experimental import pallas as pl
from jax.experimental.pallas import tpu as pltpu
from jax.sharding import PartitionSpec as P

HEAD = 128
TOK = 192
GROUPS = 2
PER_GROUP = 16
SLOTS = 16
KEYS = SLOTS * TOK
PART = 4
PARTS = PER_GROUP // PART
BLOCKS = GROUPS * PARTS
ROWS = PART * TOK
CHUNK = 1536
EDGE = 256
OWN_TOK = 48
MINUS = -1e30
SCALE = HEAD**-0.5 * math.log2(math.e)
MESH = pl.DeviceIdType.MESH


PLANES = 2 * GROUPS
MOVES = 3


def rows_of(slot):
    return pl.ds(pl.multiple_of(slot * TOK, TOK), TOK)


def kernel(
    q_hbm, k_hbm, v_hbm, len_ref, out_ref,
    kv, s_ref, top_ref, m_ref, near_ref, total_ref, qv, qs, ob, row_bias_ref, key_bias_ref, bias_ref,
    in_sem, above_sem, send_sem, recv_sem, osend_sem, orecv_sem, olocal_sem,
):
    ctx = lax.axis_index("ctx")
    y = lax.axis_index("head")
    z = ctx // 8
    x = lax.rem(ctx // 2, 4)
    c = lax.rem(ctx, 2)

    def place(z_at, x_at, c_at):
        return (lax.rem(z_at + 8, 8) * 8 + x_at * 2 + c_at, y)

    sibling = place(z, x, 1 - c)
    others = [lax.rem(x + r, 4) for r in (1, 3, 2)]
    over_x = [place(z, to, c) for to in others]
    over_y = [(ctx, lax.rem(y + r, 4)) for r in (1, 2, 3)]
    loads = []
    for p in range(PLANES):
        loads.append(pltpu.make_async_copy(
            (k_hbm, v_hbm)[p % 2].at[:, pl.ds(p // 2 * HEAD, HEAD)],
            kv.at[p, pl.ds(0, TOK), :], in_sem.at[p]))
    q_load = pltpu.make_async_copy(q_hbm, qv, in_sem.at[PLANES])
    for load in loads:
        load.start()
    q_load.start()

    barrier = pltpu.get_barrier_semaphore()
    above, below = place(z + 1, x, c), place(z - 1, x, c)
    has_above, has_below = z < 7, z > 0
    aslant = [place(z + 1, to, c) for to in others]
    from_slant = [place(z - 1, to, c) for to in others]
    partners = [sibling] + over_x + over_y
    for partner in partners:
        pl.semaphore_signal(barrier, inc=1, device_id=partner, device_id_type=MESH)

    @pl.when(has_above)
    def _():
        pl.semaphore_signal(barrier, inc=1, device_id=above, device_id_type=MESH)
        for r in range(3):
            @pl.when(others[r] < x)
            def _():
                pl.semaphore_signal(barrier, inc=1, device_id=aslant[r], device_id_type=MESH)

    pl.semaphore_wait(barrier, len(partners) + jnp.where(has_below, 4 - x, 0))

    @pl.when(has_below)
    def _():
        pl.semaphore_signal(above_sem, inc=1, device_id=below, device_id_type=MESH)
        for r in range(3):
            @pl.when(others[r] > x)
            def _():
                pl.semaphore_signal(above_sem, inc=1, device_id=from_slant[r], device_id_type=MESH)

    for load in loads:
        load.wait()

    def copy(p, index, src, dst, target):
        planes = pl.ds(p, 1 if p < 2 else 2)
        return pltpu.make_async_remote_copy(
            src_ref=kv.at[planes, rows_of(src), :], dst_ref=kv.at[planes, rows_of(dst), :],
            send_sem=send_sem.at[p, index], recv_sem=recv_sem.at[p, dst],
            device_id=target, device_id_type=MESH)

    def arrived(p, slot):
        copy(p, 0, slot, slot, sibling).wait_recv()

    def z_one(p): return copy(p, 0, 0, 8, above)
    def z_two(p): return copy(p, 1, 8, 16, above)

    def even(p, r):
        to = others[r]
        return copy(p, 2 + r, jnp.where(to > x, 0, 16), lax.rem(2 * (to - x) + 16, 16), over_x[r])

    def back(p, r):
        return copy(p, 5 + r, 8, 8 + 2 * (others[r] - x), over_x[r])

    def slanted(r):
        return copy(0, 5 + r, 0, 8 + 2 * (others[r] - x), aslant[r])

    def aside(p, slot): return copy(p, 8 + slot // 2, slot, slot + 1 - 2 * c, sibling)
    def aside_own(p): return copy(p, 8, 16 * c, 1 + 14 * c, sibling)

    def send_up(*planes):
        @pl.when(has_above)
        def _():
            for p in planes:
                z_one(p).start()

    def send_slanted():
        @pl.when(has_above)
        def _():
            for r in range(3):
                @pl.when(others[r] < x)
                def _():
                    slanted(r).start()

    def send_row(p):
        for r in range(3):
            @pl.when(others[r] > x)
            def _():
                even(p, r).start()

        @pl.when(c == 0)
        def _():
            aside_own(p).start()

    def pass_up(p):
        @pl.when(has_below)
        def _():
            arrived(p, 8)

            @pl.when(has_above)
            def _():
                z_two(p).start()

    def back_near(p):
        @pl.when(has_below)
        def _():
            aside(p, 8).start()
            if p > 0:
                for r in range(3):
                    @pl.when(others[r] < x)
                    def _():
                        back(p, r).start()

    def back_far(p):
        @pl.when(has_below)
        def _():
            for r in range(3):
                @pl.when(others[r] > x)
                def _():
                    back(p, r).start()

    def send_old(p):
        @pl.when(z > 1)
        def _():
            arrived(p, 16)
            for r in range(3):
                @pl.when(others[r] < x)
                def _():
                    even(p, r).start()

            @pl.when(c == 1)
            def _():
                aside_own(p).start()

    def share(p, slots):
        for slot in slots:
            @pl.when(ctx >= slot)
            def _():
                arrived(p, slot)
                aside(p, slot).start()

    def await_odd(p, slots):
        for slot in slots:
            @pl.when(ctx >= slot)
            def _():
                arrived(p, slot)

    def sent(p):
        @pl.when(has_above)
        def _():
            z_one(p).wait_send()

        @pl.when(has_above & has_below)
        def _():
            z_two(p).wait_send()

        for r in range(3):
            by_slant = others[r] < x if p == 0 else False

            @pl.when(has_above & by_slant | has_below & jnp.logical_not(by_slant))
            def _():
                back(p, r).wait_send()
        for r in range(3):
            @pl.when((others[r] > x) | (z > 1))
            def _():
                even(p, r).wait_send()

        @pl.when((c == 0) | (z > 1))
        def _():
            aside_own(p).wait_send()
        for slot in range(2, 16, 2):
            @pl.when(ctx >= slot)
            def _():
                aside(p, slot).wait_send()

    def documents():
        base = ctx * TOK
        lens = jnp.broadcast_to(len_ref[...].astype(jnp.float32), (128, 128))
        row = lax.broadcasted_iota(jnp.int32, (128, 128), 0)
        col = lax.broadcasted_iota(jnp.int32, (128, 128), 1)
        ends = jnp.sum(jnp.where(row <= col, lens.T, 0.0), axis=0, keepdims=True)
        here = (base + lax.broadcasted_iota(jnp.int32, (TOK, 128), 0)).astype(jnp.float32)
        start = jnp.max(jnp.where(ends <= here, ends, 0.0), axis=1, keepdims=True)
        offset = start - base.astype(jnp.float32)
        rest = jnp.broadcast_to(jnp.where(offset < 0.0, 0.0, MINUS), (TOK, 128))
        row_bias_ref[...] = rest
        col = lax.broadcasted_iota(jnp.int32, (8, KEYS), 1)
        slot = col // TOK
        at = (col - 2 * TOK * slot).astype(jnp.float32)
        key_bias_ref[...] = jnp.where(at >= offset[:8], 0.0, MINUS)[0:1]
        i = lax.broadcasted_iota(jnp.int32, (TOK, EDGE), 0)
        j = lax.broadcasted_iota(jnp.int32, (TOK, EDGE), 1)
        inside = (j <= i) & (j.astype(jnp.float32) >= offset)
        rest = jnp.concatenate([rest, rest], axis=1) + key_bias_ref[:, :EDGE]
        bias_ref[...] = jnp.where(j < TOK, jnp.where(inside, 0.0, MINUS), rest)

    def clear():
        def one(slot, carry):
            @pl.when(ctx < slot)
            def _():
                for p in range(PLANES):
                    kv[p, rows_of(slot), :] = jnp.zeros((TOK, HEAD), jnp.bfloat16)
            return carry

        lax.fori_loop(1, SLOTS, one, 0)

    def scale_queries():
        def one(h, carry):
            scaled = qv[:, pl.ds(pl.multiple_of(h * HEAD, HEAD), HEAD)].astype(jnp.float32) * SCALE
            high = scaled.astype(jnp.bfloat16)
            qs[rows_of(h), 0:HEAD] = high
            qs[rows_of(h), HEAD:] = (scaled - high.astype(jnp.float32)).astype(jnp.bfloat16)
            return carry

        lax.fori_loop(0, GROUPS * PER_GROUP, one, 0)

    def out_copies(b, head, count):
        width = count * HEAD
        cols = pl.ds(head * HEAD, width)
        at = pl.ds(pl.multiple_of(y * 4096 + (b * PART + head) * HEAD, width), width)

        def part(to):
            return ob.at[b, pl.ds(pl.multiple_of(to * OWN_TOK, 16), OWN_TOK), cols]

        copies = [pltpu.make_async_copy(part(y), out_ref.at[:, at], olocal_sem)]
        for r in range(3):
            copies.append(pltpu.make_async_remote_copy(
                src_ref=part(over_y[r][1]), dst_ref=out_ref.at[:, at],
                send_sem=osend_sem.at[r], recv_sem=orecv_sem.at[r],
                device_id=over_y[r], device_id_type=MESH))
        return copies

    def score(b, lo, hi):
        g = b // PARTS
        kept_at = lax.rem(b, PARTS)
        into = kept_at if lo < CHUNK else PARTS
        q = qs[pl.ds(pl.multiple_of(b * ROWS, ROWS), ROWS), :]
        k = kv[2 * g, lo:hi, :]
        k = jnp.concatenate([k, k], axis=1)
        s = lax.dot_general(q, k, (((1,), (1,)), ((), ())), preferred_element_type=jnp.float32)
        row_bias = jnp.concatenate([row_bias_ref[...]] * PART, axis=0)
        if lo == 0:
            edge_bias = jnp.concatenate([bias_ref[...]] * PART, axis=0)
            top = jnp.full((ROWS, 128), MINUS, jnp.float32)
        else:
            top = top_ref[kept_at]
        for u in range(lo, hi, 128):
            if u < EDGE:
                bias = edge_bias[:, u:u + 128]
            else:
                bias = row_bias + key_bias_ref[:, u:u + 128]
            masked = s[:, u - lo:u - lo + 128] + bias
            s_ref[into, :, u % CHUNK:u % CHUNK + 128] = masked
            top = jnp.maximum(top, masked)
        top_ref[kept_at] = top

    def mixed(g, t, scores, m):
        p = jnp.exp2(scores - m).astype(jnp.bfloat16)
        v = kv[2 * g + 1, t * CHUNK:(t + 1) * CHUNK, :]
        v = jnp.concatenate([v, jnp.ones_like(v)], axis=1)
        return jnp.dot(p, v, preferred_element_type=jnp.float32)

    def steps(b, table):
        for when, what in table:
            @pl.when(b == when)
            def _():
                what()

    def scores(table, lo, hi):
        def one(b, carry):
            steps(b, table)
            score(b, lo, hi)
            return carry
        return one

    def near_mix(b, carry):
        steps(b, MIX_STEPS)
        m = jnp.max(top_ref[b], axis=1, keepdims=True)
        m_ref[b] = jnp.broadcast_to(m, (ROWS, 128))
        near_ref[b] = mixed(0, 0, s_ref[b], m)
        return carry

    def block(b, carry):
        steps(b, STEPS)
        g = b // PARTS
        kept_at = lax.rem(b, PARTS)
        score(b, CHUNK, KEYS)
        steps(b, VALUE_STEPS)

        @pl.when(b < PARTS)
        def _():
            m = jnp.max(top_ref[kept_at], axis=1, keepdims=True)
            scale = jnp.exp2(m_ref[kept_at] - m)
            total_ref[:, :HEAD] = near_ref[kept_at, :, :HEAD] * scale
            total_ref[:, HEAD:] = near_ref[kept_at, :, HEAD:] * scale

        @pl.when(b >= PARTS)
        def _():
            m = jnp.max(top_ref[kept_at], axis=1, keepdims=True)
            total_ref[...] = mixed(g, 0, s_ref[kept_at], m)

        m = jnp.max(top_ref[kept_at], axis=1, keepdims=True)
        total = total_ref[...] + mixed(g, 1, s_ref[PARTS], m)
        o = (total[:, :HEAD] / total[:, HEAD:]).astype(jnp.bfloat16)
        for h in range(PART):
            ob[b, :, h * HEAD:(h + 1) * HEAD] = o[h * TOK:(h + 1) * TOK]
        for one in out_copies(b, 0, PART):
            one.start()
        return carry

    near, far = (2, 4, 6), (10, 12, 14)
    odd_near, odd_far = (1, 3, 5, 7), (9, 11, 13, 15)
    SCORE_STEPS = (
        (0, lambda: (back_far(0), send_up(2))),
        (1, lambda: (pass_up(1), back_near(1))),
        (2, lambda: send_old(0)),
        (3, lambda: (share(1, near), back_far(1))),
    )
    MIX_STEPS = (
        (0, lambda: (await_odd(1, odd_near), send_row(2))),
        (1, lambda: (send_old(1), share(0, far))),
        (2, lambda: (pass_up(2), back_near(2))),
        (3, lambda: (share(1, far), back_far(2))),
    )
    STEPS = (
        (0, lambda: await_odd(0, odd_far)),
        (1, lambda: send_old(2)),
        (3, lambda: share(2, near)),
        (4, lambda: await_odd(2, odd_far)),
    )
    VALUE_STEPS = (
        (0, lambda: await_odd(1, odd_far)),
    )
    LATER_STEPS = (
        (4, lambda: await_odd(2, odd_near)),
        (5, lambda: share(2, far)),
    )

    send_row(0)

    @pl.when(has_above)
    def _():
        pl.semaphore_wait(above_sem, x + 1)

    send_up(0)
    send_slanted()
    send_up(1)
    documents()
    clear()
    q_load.wait()
    scale_queries()
    pass_up(0)
    back_near(0)
    send_row(1)
    share(0, near)
    await_odd(0, odd_near)
    lax.fori_loop(0, PARTS, scores(SCORE_STEPS, 0, CHUNK), 0)
    lax.fori_loop(0, PARTS, near_mix, 0)
    lax.fori_loop(0, PARTS, block, 0)
    lax.fori_loop(PARTS, BLOCKS, scores(LATER_STEPS, 0, CHUNK), 0)
    lax.fori_loop(PARTS, BLOCKS, block, 0)

    mine = out_ref.at[:, pl.ds(pl.multiple_of(y * 4096, 4096), 4096)]
    for r in range(3):
        every = pltpu.make_async_remote_copy(
            src_ref=mine, dst_ref=mine, send_sem=osend_sem.at[r], recv_sem=orecv_sem.at[r],
            device_id=over_y[r], device_id_type=MESH)
        every.wait_send()
        every.wait_recv()
    pltpu.make_async_copy(mine, mine, olocal_sem).wait()
    for p in range(MOVES):
        sent(p)


def per_device(queries, keys, values, doc_lengths):
    hbm = pl.BlockSpec(memory_space=pl.ANY)
    bf16, f32 = jnp.bfloat16, jnp.float32
    return pl.pallas_call(
        kernel,
        out_shape=pltpu.VMEM((OWN_TOK, 4 * queries.shape[1]), bf16),
        in_specs=[hbm, hbm, hbm, pl.BlockSpec(memory_space=pltpu.VMEM)],
        out_specs=pl.BlockSpec(memory_space=pltpu.VMEM),
        scratch_shapes=[
            pltpu.VMEM((PLANES, (SLOTS + 1) * TOK, HEAD), bf16),
            pltpu.VMEM((PARTS + 1, ROWS, CHUNK), f32),
            pltpu.VMEM((PARTS, ROWS, 128), f32),
            pltpu.VMEM((PARTS, ROWS, 128), f32),
            pltpu.VMEM((PARTS, ROWS, 2 * HEAD), f32),
            pltpu.VMEM((ROWS, 2 * HEAD), f32),
            pltpu.VMEM((TOK, 4096), bf16),
            pltpu.VMEM((GROUPS * PER_GROUP * TOK, 2 * HEAD), bf16),
            pltpu.VMEM((BLOCKS, TOK, PART * HEAD), bf16),
            pltpu.VMEM((TOK, 128), f32),
            pltpu.VMEM((1, KEYS), f32),
            pltpu.VMEM((TOK, EDGE), f32),
            pltpu.SemaphoreType.DMA((PLANES + 1,)),
            pltpu.SemaphoreType.REGULAR,
            pltpu.SemaphoreType.DMA((MOVES, 16)),
            pltpu.SemaphoreType.DMA((MOVES, SLOTS + 1)),
            pltpu.SemaphoreType.DMA((3,)),
            pltpu.SemaphoreType.DMA((3,)),
            pltpu.SemaphoreType.DMA,
        ],
        compiler_params=pltpu.CompilerParams(
            collective_id=0, has_side_effects=True, vmem_limit_bytes=56 << 20),
    )(queries, keys, values, doc_lengths.reshape(1, 128))


def solution(mesh):
    placed = (P("ctx", "head"), P("ctx", "head"), P("ctx", "head"), P())
    return jax.shard_map(
        per_device, mesh=mesh, in_specs=placed, out_specs=P(("ctx", "head"), None), check_vma=False
    )
```

```python
import math

import jax
import jax.numpy as jnp
from jax import lax
from jax.experimental import pallas as pl
from jax.experimental.pallas import tpu as pltpu
from jax.sharding import PartitionSpec as P

HEAD = 128
TOK = 192
GROUPS = 2
PER_GROUP = 16
SLOTS = 16
KEYS = SLOTS * TOK
PART = 4
PARTS = PER_GROUP // PART
BLOCKS = GROUPS * PARTS
ROWS = PART * TOK
CHUNK = 1536
EDGE = 256
OWN_TOK = 48
MINUS = -1e30
SCALE = HEAD**-0.5 * math.log2(math.e)
MESH = pl.DeviceIdType.MESH


PLANES = 2 * GROUPS
MOVES = 3


def rows_of(slot):
    return pl.ds(pl.multiple_of(slot * TOK, TOK), TOK)


def kernel(
    q_hbm, k_hbm, v_hbm, len_ref, out_ref,
    kv, s_ref, top_ref, m_ref, near_ref, total_ref, qv, qs, ob, row_bias_ref, key_bias_ref, bias_ref,
    in_sem, send_sem, recv_sem, osend_sem, orecv_sem, olocal_sem,
):
    ctx = lax.axis_index("ctx")
    y = lax.axis_index("head")
    z = ctx // 8
    x = lax.rem(ctx // 2, 4)
    c = lax.rem(ctx, 2)

    def place(z_at, x_at, c_at):
        return (lax.rem(z_at + 8, 8) * 8 + x_at * 2 + c_at, y)

    sibling = place(z, x, 1 - c)
    others = [lax.rem(x + r, 4) for r in (1, 3, 2)]
    over_x = [place(z, to, c) for to in others]
    over_y = [(ctx, lax.rem(y + r, 4)) for r in (1, 2, 3)]
    loads = []
    for p in range(PLANES):
        loads.append(pltpu.make_async_copy(
            (k_hbm, v_hbm)[p % 2].at[:, pl.ds(p // 2 * HEAD, HEAD)],
            kv.at[p, pl.ds(0, TOK), :], in_sem.at[p]))
    q_load = pltpu.make_async_copy(q_hbm, qv, in_sem.at[PLANES])
    for load in loads:
        load.start()
    q_load.start()

    barrier = pltpu.get_barrier_semaphore()
    above, below = place(z + 1, x, c), place(z - 1, x, c)
    has_above, has_below = z < 7, z > 0
    aslant = [place(z + 1, to, c) for to in others]
    from_slant = [place(z - 1, to, c) for to in others]
    partners = [sibling] + over_x + over_y
    for partner in partners:
        pl.semaphore_signal(barrier, inc=1, device_id=partner, device_id_type=MESH)

    @pl.when(has_above)
    def _():
        pl.semaphore_signal(barrier, inc=1, device_id=above, device_id_type=MESH)
        for r in range(3):
            @pl.when(others[r] < x)
            def _():
                pl.semaphore_signal(barrier, inc=1, device_id=aslant[r], device_id_type=MESH)

    @pl.when(has_below)
    def _():
        pl.semaphore_signal(barrier, inc=1, device_id=below, device_id_type=MESH)
        for r in range(3):
            @pl.when(others[r] > x)
            def _():
                pl.semaphore_signal(barrier, inc=1, device_id=from_slant[r], device_id_type=MESH)

    pl.semaphore_wait(
        barrier, len(partners) + jnp.where(has_below, 4 - x, 0) + jnp.where(has_above, x + 1, 0))

    for load in loads:
        load.wait()

    def copy(p, index, src, dst, target):
        planes = pl.ds(p, 1 if p < 2 else 2)
        return pltpu.make_async_remote_copy(
            src_ref=kv.at[planes, rows_of(src), :], dst_ref=kv.at[planes, rows_of(dst), :],
            send_sem=send_sem.at[p, index], recv_sem=recv_sem.at[p, dst],
            device_id=target, device_id_type=MESH)

    def arrived(p, slot):
        copy(p, 0, slot, slot, sibling).wait_recv()

    def z_one(p): return copy(p, 0, 0, 8, above)
    def z_two(p): return copy(p, 1, 8, 16, above)

    def even(p, r):
        to = others[r]
        return copy(p, 2 + r, jnp.where(to > x, 0, 16), lax.rem(2 * (to - x) + 16, 16), over_x[r])

    def back(p, r):
        return copy(p, 5 + r, 8, 8 + 2 * (others[r] - x), over_x[r])

    def slanted(r):
        return copy(0, 5 + r, 0, 8 + 2 * (others[r] - x), aslant[r])

    def aside(p, slot): return copy(p, 8 + slot // 2, slot, slot + 1 - 2 * c, sibling)
    def aside_own(p): return copy(p, 8, 16 * c, 1 + 14 * c, sibling)

    def send_up(*planes):
        @pl.when(has_above)
        def _():
            for p in planes:
                z_one(p).start()

    def send_slanted():
        @pl.when(has_above)
        def _():
            for r in range(3):
                @pl.when(others[r] < x)
                def _():
                    slanted(r).start()

    def send_row(p):
        for r in range(3):
            @pl.when(others[r] > x)
            def _():
                even(p, r).start()

        @pl.when(c == 0)
        def _():
            aside_own(p).start()

    def pass_up(p):
        @pl.when(has_below)
        def _():
            arrived(p, 8)

            @pl.when(has_above)
            def _():
                z_two(p).start()

    def back_near(p):
        @pl.when(has_below)
        def _():
            aside(p, 8).start()
            if p > 0:
                for r in range(3):
                    @pl.when(others[r] < x)
                    def _():
                        back(p, r).start()

    def back_far(p):
        @pl.when(has_below)
        def _():
            for r in range(3):
                @pl.when(others[r] > x)
                def _():
                    back(p, r).start()

    def send_old(p):
        @pl.when(z > 1)
        def _():
            arrived(p, 16)
            for r in range(3):
                @pl.when(others[r] < x)
                def _():
                    even(p, r).start()

            @pl.when(c == 1)
            def _():
                aside_own(p).start()

    def share(p, slots):
        for slot in slots:
            @pl.when(ctx >= slot)
            def _():
                arrived(p, slot)
                aside(p, slot).start()

    def await_odd(p, slots):
        for slot in slots:
            @pl.when(ctx >= slot)
            def _():
                arrived(p, slot)

    def sent(p):
        @pl.when(has_above)
        def _():
            z_one(p).wait_send()

        @pl.when(has_above & has_below)
        def _():
            z_two(p).wait_send()

        for r in range(3):
            by_slant = others[r] < x if p == 0 else False

            @pl.when(has_above & by_slant | has_below & jnp.logical_not(by_slant))
            def _():
                back(p, r).wait_send()
        for r in range(3):
            @pl.when((others[r] > x) | (z > 1))
            def _():
                even(p, r).wait_send()

        @pl.when((c == 0) | (z > 1))
        def _():
            aside_own(p).wait_send()
        for slot in range(2, 16, 2):
            @pl.when(ctx >= slot)
            def _():
                aside(p, slot).wait_send()

    def documents():
        base = ctx * TOK
        lens = jnp.broadcast_to(len_ref[...].astype(jnp.float32), (128, 128))
        row = lax.broadcasted_iota(jnp.int32, (128, 128), 0)
        col = lax.broadcasted_iota(jnp.int32, (128, 128), 1)
        ends = jnp.sum(jnp.where(row <= col, lens.T, 0.0), axis=0, keepdims=True)
        here = (base + lax.broadcasted_iota(jnp.int32, (TOK, 128), 0)).astype(jnp.float32)
        start = jnp.max(jnp.where(ends <= here, ends, 0.0), axis=1, keepdims=True)
        offset = start - base.astype(jnp.float32)
        rest = jnp.broadcast_to(jnp.where(offset < 0.0, 0.0, MINUS), (TOK, 128))
        row_bias_ref[...] = rest
        col = lax.broadcasted_iota(jnp.int32, (8, KEYS), 1)
        slot = col // TOK
        at = (col - 2 * TOK * slot).astype(jnp.float32)
        key_bias_ref[...] = jnp.where(at >= offset[:8], 0.0, MINUS)[0:1]
        i = lax.broadcasted_iota(jnp.int32, (TOK, EDGE), 0)
        j = lax.broadcasted_iota(jnp.int32, (TOK, EDGE), 1)
        inside = (j <= i) & (j.astype(jnp.float32) >= offset)
        rest = jnp.concatenate([rest, rest], axis=1) + key_bias_ref[:, :EDGE]
        bias_ref[...] = jnp.where(j < TOK, jnp.where(inside, 0.0, MINUS), rest)

    def clear():
        def one(slot, carry):
            @pl.when(ctx < slot)
            def _():
                for p in range(PLANES):
                    kv[p, rows_of(slot), :] = jnp.zeros((TOK, HEAD), jnp.bfloat16)
            return carry

        lax.fori_loop(1, SLOTS, one, 0)

    def scale_queries():
        def one(h, carry):
            scaled = qv[:, pl.ds(pl.multiple_of(h * HEAD, HEAD), HEAD)].astype(jnp.float32) * SCALE
            high = scaled.astype(jnp.bfloat16)
            qs[rows_of(h), 0:HEAD] = high
            qs[rows_of(h), HEAD:] = (scaled - high.astype(jnp.float32)).astype(jnp.bfloat16)
            return carry

        lax.fori_loop(0, GROUPS * PER_GROUP, one, 0)

    def out_copies(b, head, count):
        width = count * HEAD
        cols = pl.ds(head * HEAD, width)
        at = pl.ds(pl.multiple_of(y * 4096 + (b * PART + head) * HEAD, width), width)

        def part(to):
            return ob.at[b, pl.ds(pl.multiple_of(to * OWN_TOK, 16), OWN_TOK), cols]

        copies = [pltpu.make_async_copy(part(y), out_ref.at[:, at], olocal_sem)]
        for r in range(3):
            copies.append(pltpu.make_async_remote_copy(
                src_ref=part(over_y[r][1]), dst_ref=out_ref.at[:, at],
                send_sem=osend_sem.at[r], recv_sem=orecv_sem.at[r],
                device_id=over_y[r], device_id_type=MESH))
        return copies

    def score(b, lo, hi):
        g = b // PARTS
        kept_at = lax.rem(b, PARTS)
        into = kept_at if lo < CHUNK else PARTS
        q = qs[pl.ds(pl.multiple_of(b * ROWS, ROWS), ROWS), :]
        k = kv[2 * g, lo:hi, :]
        k = jnp.concatenate([k, k], axis=1)
        s = lax.dot_general(q, k, (((1,), (1,)), ((), ())), preferred_element_type=jnp.float32)
        row_bias = jnp.concatenate([row_bias_ref[...]] * PART, axis=0)
        if lo == 0:
            edge_bias = jnp.concatenate([bias_ref[...]] * PART, axis=0)
            top = jnp.full((ROWS, 128), MINUS, jnp.float32)
        else:
            top = top_ref[kept_at]
        for u in range(lo, hi, 128):
            if u < EDGE:
                bias = edge_bias[:, u:u + 128]
            else:
                bias = row_bias + key_bias_ref[:, u:u + 128]
            masked = s[:, u - lo:u - lo + 128] + bias
            s_ref[into, :, u % CHUNK:u % CHUNK + 128] = masked
            top = jnp.maximum(top, masked)
        top_ref[kept_at] = top

    def mixed(g, t, scores, m):
        p = jnp.exp2(scores - m).astype(jnp.bfloat16)
        v = kv[2 * g + 1, t * CHUNK:(t + 1) * CHUNK, :]
        v = jnp.concatenate([v, jnp.ones_like(v)], axis=1)
        return jnp.dot(p, v, preferred_element_type=jnp.float32)

    def steps(b, table):
        for when, what in table:
            @pl.when(b == when)
            def _():
                what()

    def scores(table, lo, hi):
        def one(b, carry):
            steps(b, table)
            score(b, lo, hi)
            return carry
        return one

    def near_mix(b, carry):
        steps(b, MIX_STEPS)
        m = jnp.max(top_ref[b], axis=1, keepdims=True)
        m_ref[b] = jnp.broadcast_to(m, (ROWS, 128))
        near_ref[b] = mixed(0, 0, s_ref[b], m)
        return carry

    def block(b, carry):
        steps(b, STEPS)
        g = b // PARTS
        kept_at = lax.rem(b, PARTS)
        score(b, CHUNK, KEYS)
        steps(b, VALUE_STEPS)

        @pl.when(b < PARTS)
        def _():
            m = jnp.max(top_ref[kept_at], axis=1, keepdims=True)
            scale = jnp.exp2(m_ref[kept_at] - m)
            total_ref[:, :HEAD] = near_ref[kept_at, :, :HEAD] * scale
            total_ref[:, HEAD:] = near_ref[kept_at, :, HEAD:] * scale

        @pl.when(b >= PARTS)
        def _():
            m = jnp.max(top_ref[kept_at], axis=1, keepdims=True)
            total_ref[...] = mixed(g, 0, s_ref[kept_at], m)

        m = jnp.max(top_ref[kept_at], axis=1, keepdims=True)
        total = total_ref[...] + mixed(g, 1, s_ref[PARTS], m)
        o = (total[:, :HEAD] / total[:, HEAD:]).astype(jnp.bfloat16)
        for h in range(PART):
            ob[b, :, h * HEAD:(h + 1) * HEAD] = o[h * TOK:(h + 1) * TOK]
        for one in out_copies(b, 0, PART):
            one.start()
        return carry

    near, far = (2, 4, 6), (10, 12, 14)
    odd_near, odd_far = (1, 3, 5, 7), (9, 11, 13, 15)
    SCORE_STEPS = (
        (0, lambda: (back_far(0), send_up(2))),
        (1, lambda: (pass_up(1), back_near(1))),
        (2, lambda: send_old(0)),
        (3, lambda: (share(1, near), back_far(1))),
    )
    MIX_STEPS = (
        (0, lambda: (await_odd(1, odd_near), send_row(2))),
        (1, lambda: (send_old(1), share(0, far))),
        (2, lambda: (pass_up(2), back_near(2))),
        (3, lambda: (share(1, far), back_far(2))),
    )
    STEPS = (
        (0, lambda: await_odd(0, odd_far)),
        (1, lambda: send_old(2)),
        (3, lambda: share(2, near)),
        (4, lambda: await_odd(2, odd_far)),
    )
    VALUE_STEPS = (
        (0, lambda: await_odd(1, odd_far)),
    )
    LATER_STEPS = (
        (4, lambda: await_odd(2, odd_near)),
        (5, lambda: share(2, far)),
    )

    send_up(0)
    send_slanted()
    send_row(0)
    send_up(1)
    documents()
    clear()
    q_load.wait()
    scale_queries()
    pass_up(0)
    back_near(0)
    send_row(1)
    share(0, near)
    await_odd(0, odd_near)
    lax.fori_loop(0, PARTS, scores(SCORE_STEPS, 0, CHUNK), 0)
    lax.fori_loop(0, PARTS, near_mix, 0)
    lax.fori_loop(0, PARTS, block, 0)
    lax.fori_loop(PARTS, BLOCKS, scores(LATER_STEPS, 0, CHUNK), 0)
    lax.fori_loop(PARTS, BLOCKS, block, 0)

    mine = out_ref.at[:, pl.ds(pl.multiple_of(y * 4096, 4096), 4096)]
    for r in range(3):
        every = pltpu.make_async_remote_copy(
            src_ref=mine, dst_ref=mine, send_sem=osend_sem.at[r], recv_sem=orecv_sem.at[r],
            device_id=over_y[r], device_id_type=MESH)
        every.wait_send()
        every.wait_recv()
    pltpu.make_async_copy(mine, mine, olocal_sem).wait()
    for p in range(MOVES):
        sent(p)


def per_device(queries, keys, values, doc_lengths):
    hbm = pl.BlockSpec(memory_space=pl.ANY)
    bf16, f32 = jnp.bfloat16, jnp.float32
    return pl.pallas_call(
        kernel,
        out_shape=pltpu.VMEM((OWN_TOK, 4 * queries.shape[1]), bf16),
        in_specs=[hbm, hbm, hbm, pl.BlockSpec(memory_space=pltpu.VMEM)],
        out_specs=pl.BlockSpec(memory_space=pltpu.VMEM),
        scratch_shapes=[
            pltpu.VMEM((PLANES, (SLOTS + 1) * TOK, HEAD), bf16),
            pltpu.VMEM((PARTS + 1, ROWS, CHUNK), f32),
            pltpu.VMEM((PARTS, ROWS, 128), f32),
            pltpu.VMEM((PARTS, ROWS, 128), f32),
            pltpu.VMEM((PARTS, ROWS, 2 * HEAD), f32),
            pltpu.VMEM((ROWS, 2 * HEAD), f32),
            pltpu.VMEM((TOK, 4096), bf16),
            pltpu.VMEM((GROUPS * PER_GROUP * TOK, 2 * HEAD), bf16),
            pltpu.VMEM((BLOCKS, TOK, PART * HEAD), bf16),
            pltpu.VMEM((TOK, 128), f32),
            pltpu.VMEM((1, KEYS), f32),
            pltpu.VMEM((TOK, EDGE), f32),
            pltpu.SemaphoreType.DMA((PLANES + 1,)),
            pltpu.SemaphoreType.DMA((MOVES, 16)),
            pltpu.SemaphoreType.DMA((MOVES, SLOTS + 1)),
            pltpu.SemaphoreType.DMA((3,)),
            pltpu.SemaphoreType.DMA((3,)),
            pltpu.SemaphoreType.DMA,
        ],
        compiler_params=pltpu.CompilerParams(
            collective_id=0, has_side_effects=True, vmem_limit_bytes=56 << 20),
    )(queries, keys, values, doc_lengths.reshape(1, 128))


def solution(mesh):
    placed = (P("ctx", "head"), P("ctx", "head"), P("ctx", "head"), P())
    return jax.shard_map(
        per_device, mesh=mesh, in_specs=placed, out_specs=P(("ctx", "head"), None), check_vma=False
    )
```
